512 devices in a mesh: wide: 128 (over z, y, core), narrow: 4 (over x).
Axes of the slice: x: 4, y: 8, z: 8, core: 2. Of those that a mesh axis runs over, the one named last changes fastest.
Arguments:
- slab: bfloat16 [98304, 2048], P('wide', 'narrow'), may hold values from -1.1953125 to 1.1953125
- occupation: float32 [4096], replicated, may hold values from 0.02 to 2
- column_band: int32 [2048], P('narrow'), may hold values from 0 to 4095
- pattern: int32 [768, 12], P('wide'), may hold values from 0 to 767, as said below
Outputs:
- density: bfloat16 [768, 12, 128, 128], P('wide', 'narrow')
The draws below stay inside these ranges and needn't reach their ends.
Inputs may be any that keep to these rules, and one draw needn't show every extreme that they name: `pattern`: each row c lists 12 different clusters, each equal to (c + d) mod 768 with -8 <= d <= 8; d = -8 and d = 8 appear in every row.
All inputs are finite; a program needn't handle non-finite values.
Results may differ from the reference program's by a relative error of at most 0.015.
Values may be sent and summed in bfloat16 or wider, within the bound.
A program may use at most 64 MiB of HBM per device.

```python
import math
import jax
import jax.numpy as jnp
from jax import lax

B = 128
K = 2048
NBAND = 4096
NNB = 12
REACH = 8
NCL = 768
ORB = 98304
N_NARROW = 4


def draw_pattern(key, part):
    key = jax.random.fold_in(key, 7)
    keys = jax.random.split(key, NCL)
    inner = jax.vmap(lambda k: jax.random.permutation(k, 2 * REACH - 1))(keys)
    inner = inner[:, :NNB - 2] - (REACH - 1)
    edges = jnp.broadcast_to(jnp.array([-REACH, REACH], dtype=jnp.int32), (NCL, 2))
    offsets = jnp.concatenate([edges, inner.astype(jnp.int32)], axis=1)
    rows = jnp.arange(NCL, dtype=jnp.int32)[:, None]
    return ((rows + offsets) % NCL).astype(jnp.int32)


def with_ends(values, stream_key, least, top_value):
    spot = [jax.random.randint(jax.random.fold_in(stream_key, axis), (), 0, length) for axis, length in enumerate(values.shape)]
    main_axis = values.shape.index(max(values.shape))
    beside = spot[:main_axis] + [(spot[main_axis] + 1) % values.shape[main_axis]] + spot[main_axis + 1:]
    return values.at[tuple(spot)].set(least).at[tuple(beside)].set(top_value)


def level_of(key, shape, cuts, least, high):
    def one(axis_at, shards_of):
        steps = jax.random.uniform(jax.random.fold_in(jax.random.fold_in(key, 6), axis_at), (shards_of,), jnp.float32, least / len(cuts), high / len(cuts))
        return jnp.repeat(jnp.exp(steps), shape[axis_at] // shards_of).reshape((-1,) + (1,) * (len(shape) - axis_at - 1))

    gain = one(*cuts[0])
    for cut in cuts[1:]:
        gain = gain * one(*cut)
    return gain


def gaussian(key, shape, spread, most, shards=(), kind=jnp.bfloat16):
    drawn = jax.random.normal(key, shape, jnp.float32) * spread
    if len(shards) > 0:
        drawn = level_of(key, shape, shards, -0.22, 0.18) * drawn
    return jnp.clip(drawn, min=-most, max=most).astype(kind)


def setup_inputs(seed: int = 0) -> dict:
    splits = jax.random.split(jax.random.key(seed), 5)
    slab = gaussian(splits[0], (ORB, K), 0.2, 1.1953125, ((0, 128), (1, 4)))
    occupation = jnp.clip(jnp.exp(jax.random.uniform(splits[1], (NBAND,), jnp.float32, math.log(0.02), math.log(2.0))), 0.02, 2.0)
    column_band = with_ends(jax.random.randint(splits[2], (K,), 0, NBAND), jax.random.fold_in(splits[2], 1), 0, NBAND - 1).astype(jnp.int32)
    pattern = draw_pattern(jax.random.fold_in(splits[4], 71), 0)
    return {"slab": slab, "occupation": occupation, "column_band": column_band, "pattern": pattern}


def reference(slab, occupation, column_band, pattern):
    picks = column_band[:, None] == jnp.arange(NBAND, dtype=jnp.int32)[None, :]
    weight = jnp.sum(jnp.where(picks, occupation[None, :], jnp.float32(0.0)), axis=1)
    scaled = (slab.astype(jnp.float32) * weight[None, :]).astype(jnp.bfloat16)
    quarter = K // N_NARROW
    left_all = scaled.reshape(NCL, B, N_NARROW, quarter)
    right_all = slab.reshape(NCL, B, N_NARROW, quarter)

    def one_cluster(c):
        left = left_all[c].astype(jnp.float32)
        right = jnp.take(right_all, pattern[c], axis=0).astype(jnp.float32)
        parts = jnp.einsum("iqk,njqk->qnij", left, right).astype(jnp.bfloat16)
        return jnp.sum(parts.astype(jnp.float32), axis=0).astype(jnp.bfloat16)

    return lax.map(one_cluster, jnp.arange(NCL, dtype=jnp.int32))
```

```python
import functools

import jax
import jax.numpy as jnp
from jax import lax
from jax.experimental import pallas as pl
from jax.experimental.pallas import tpu as pltpu
from jax.sharding import PartitionSpec as P

MESH = pl.DeviceIdType.MESH
B = 128
REACH = 8
BAND = 2 * REACH + 1
OWN = 6
WINDOW = OWN + 2 * REACH
NJ = 2
JC = B // NJ
HALF = JC // 2
JOBS = OWN * NJ
SHARE = 3


def kernel(
    n_clusters, slab, occ, band, pattern, out,
    window, scaled, blocks, parts, first_up, first_down, sum_up, sum_down, total, result,
    occ_v, band_v, pat,
    own_sem, in_sem, halo_recv, near_send, core_send, far_send, relay_send,
    up1_send, up1_recv, down1_send, down1_recv, up2_send, up2_recv, down2_send, down2_recv, out_sem,
):
    wide = lax.axis_index("wide")
    here = lax.axis_index("narrow")
    n_chips = lax.axis_size("wide") // 2
    n_narrow = lax.axis_size("narrow")
    chip, core = wide // 2, lax.rem(wide, 2)
    outward = 2 * core - 1
    near_chip = lax.rem(chip + outward + n_chips, n_chips)
    far_chip = lax.rem(chip - outward + n_chips, n_chips)
    other = (chip * 2 + 1 - core, here)
    near_other = (near_chip * 2 + 1 - core, here)
    near_same = (near_chip * 2 + core, here)
    far_same = (far_chip * 2 + core, here)
    up = (wide, lax.rem(here + 1, n_narrow))
    down = (wide, lax.rem(here + n_narrow - 1, n_narrow))

    def cluster(pos):
        return jnp.where(core == 0, pos, OWN - 1 - pos)

    own = [
        pltpu.make_async_copy(slab.at[cluster(p)], window.at[:, REACH + p], own_sem.at[p])
        for p in range(OWN)
    ]
    small = [
        pltpu.make_async_copy(occ, occ_v, in_sem.at[0]),
        pltpu.make_async_copy(band, band_v, in_sem.at[1]),
        pltpu.make_async_copy(pattern, pat, in_sem.at[2]),
    ]
    for copy in own + small:
        copy.start()

    barrier = pltpu.get_barrier_semaphore()
    for device in (other, near_other, near_same, up, down):
        pl.semaphore_signal(barrier, inc=1, device_id=device, device_id_type=MESH)
    pl.semaphore_wait(barrier, 5)

    def remote(src, dst, send_sem, recv_sem, device):
        return pltpu.make_async_remote_copy(
            src_ref=src, dst_ref=dst, send_sem=send_sem, recv_sem=recv_sem,
            device_id=device, device_id_type=MESH,
        )

    def halo(h, src, to, send_sem, device):
        return remote(src, window.at[h, to], send_sem, halo_recv.at[h, to], device)

    def near_copy(h, p):
        return halo(h, slab.at[cluster(p), h], 7 - p, near_send.at[h, p], near_other)

    def core_copy(h, p):
        return halo(h, slab.at[cluster(p), h], 19 - p, core_send.at[h, p], other)

    def far_copy(h, p):
        return halo(h, slab.at[cluster(p), h], p - 4, far_send.at[h, p - 4], far_same)

    def relay_copy(h, k):
        return halo(h, window.at[h, k], 27 - k, relay_send.at[h, 7 - k], other)

    def arrived(h, k):
        halo(h, window.at[h, k], k, relay_send.at[h, 0], other).wait_recv()

    def send_for(job):
        s, h = divmod(job, NJ)
        if s == 0:
            for p in range(3):
                near_copy(h, p).start()
        elif s <= 3:
            near_copy(h, s + 2).start()
        else:
            far_copy(h, 9 - s).start()

    with jax.named_scope("first_sends"):
        send_for(0)
        for h in range(NJ):
            for p in range(OWN):
                core_copy(h, p).start()
        send_for(1)

    with jax.named_scope("weights"):
        for copy in small:
            copy.wait()
        table = occ_v[...]
        turned = jnp.transpose(
            jnp.concatenate([table, jnp.zeros((B - table.shape[0], B), jnp.float32)], axis=0)
        )
        bands = band_v[...]
        high, low = bands // B, lax.rem(bands, B)
        cols = bands.shape[1]
        at = lax.broadcasted_iota(jnp.int32, (B, cols), 0)
        pick_high = jnp.where(at == high, 1.0, 0.0).astype(jnp.bfloat16)
        pick_low = at == low
        rest, looked = turned, jnp.zeros((B, cols), jnp.float32)
        found = []
        for _ in range(3):
            piece = rest.astype(jnp.bfloat16)
            rest = rest - piece.astype(jnp.float32)
            found.append(jnp.dot(piece, pick_high, preferred_element_type=jnp.float32))
        looked = (found[2] + found[1]) + found[0]
        weight = jnp.sum(jnp.where(pick_low, looked, 0.0), axis=0, keepdims=True)

    with jax.named_scope("scale"):
        for p in range(OWN):
            own[p].wait()
            for h in range(NJ):
                rows = window[h, REACH + p].astype(jnp.float32) * weight
                scaled[p, pl.ds(h * JC, JC)] = rows.astype(jnp.bfloat16)

    def up1(job):
        return remote(parts.at[job, 2, 0], first_up.at[job], up1_send.at[job], up1_recv.at[job], up)

    def down1(job):
        return remote(parts.at[job, 2, 1], first_down.at[job], down1_send.at[job], down1_recv.at[job], down)

    def up2(job):
        return remote(parts.at[job, 1], sum_up.at[job], up2_send.at[job], up2_recv.at[job], up)

    def down2(job):
        return remote(parts.at[job, 3], sum_down.at[job], down2_send.at[job], down2_recv.at[job], down)

    def place(job):
        s, h = divmod(job, NJ)
        return OWN - 1 - s, h

    def compute(job):
        p, h = place(job)
        right = window[h, p : p + BAND].reshape(BAND * JC, -1)
        product = lax.dot_general(
            right, scaled[p], (((1,), (1,)), ((), ())), preferred_element_type=jnp.float32
        )
        blocks[...] = product.astype(jnp.bfloat16).reshape(BAND, JC, B)
        c = cluster(p)
        mine = wide * OWN + c
        for r in (2, 1, 3, 0):
            for m in range(SHARE):
                slot = lax.rem(here + r, n_narrow) * SHARE + m
                offset = lax.rem(pat[c, slot] - mine + (REACH + n_clusters), n_clusters)
                offset = jnp.clip(offset, 0, BAND - 1)
                entry = jnp.where(core == 0, offset, BAND - 1 - offset)
                block = blocks[entry]
                parts[job, r, 0, m] = block[:HALF]
                parts[job, r, 1, m] = block[HALF:]
            if r == 2:
                up1(job).start()
                down1(job).start()

    def pass_on(job):
        up1(job).wait_recv()
        parts[job, 1, 0] = (
            parts[job, 1, 0].astype(jnp.float32) + first_up[job].astype(jnp.float32)
        ).astype(jnp.bfloat16)
        up2(job).start()
        down1(job).wait_recv()
        parts[job, 3, 1] = (
            parts[job, 3, 1].astype(jnp.float32) + first_down[job].astype(jnp.float32)
        ).astype(jnp.bfloat16)
        down2(job).start()

    def finish(job):
        p, h = place(job)
        c = cluster(p)
        up2(job).wait_recv()
        down2(job).wait_recv()
        for half in range(2):
            total[:, pl.ds(h * JC + half * HALF, HALF)] = (
                parts[job, 0, half].astype(jnp.float32)
                + sum_up[job, half].astype(jnp.float32)
                + sum_down[job, half].astype(jnp.float32)
            )
        if h == NJ - 1:
            for m in range(SHARE):
                result[c, m] = jnp.transpose(total[m]).astype(jnp.bfloat16)
            pltpu.make_async_copy(result.at[c], out.at[c], out_sem.at[p]).start()

    for job in range(JOBS):
        p, h = place(job)
        with jax.named_scope("wait_halo"):
            if job < NJ:
                for k in (7, 6):
                    arrived(h, k)
                    relay_copy(h, k).start()
                for k in (5, 14, 15, 16, 17, 18, 19, 20, 21):
                    arrived(h, k)
            else:
                arrived(h, p)
        if job + 2 < JOBS:
            send_for(job + 2)
        with jax.named_scope("blocks"):
            compute(job)
        if job >= 1:
            with jax.named_scope("pass_on"):
                pass_on(job - 1)
        if job >= 3:
            with jax.named_scope("finish"):
                finish(job - 3)
    with jax.named_scope("pass_on"):
        pass_on(JOBS - 1)
    with jax.named_scope("finish"):
        for job in range(JOBS - 3, JOBS):
            finish(job)

    with jax.named_scope("drain"):
        for h in range(NJ):
            for p in range(OWN):
                near_copy(h, p).wait_send()
                core_copy(h, p).wait_send()
            for p in (4, 5):
                far_copy(h, p).wait_send()
            for k in (7, 6):
                relay_copy(h, k).wait_send()
        for job in range(JOBS):
            up1(job).wait_send()
            down1(job).wait_send()
            up2(job).wait_send()
            down2(job).wait_send()
        for p in range(OWN):
            c = cluster(p)
            pltpu.make_async_copy(result.at[c], out.at[c], out_sem.at[p]).wait()


def per_device(slab, occupation, column_band, pattern):
    cols = slab.shape[1]
    n_clusters = OWN * lax.axis_size("wide")
    dma = pltpu.SemaphoreType.DMA
    bf16, f32 = jnp.bfloat16, jnp.float32
    return pl.pallas_call(
        functools.partial(kernel, n_clusters),
        out_shape=jax.ShapeDtypeStruct((OWN, SHARE, B, B), bf16),
        in_specs=[pl.BlockSpec(memory_space=pl.ANY)] * 4,
        out_specs=pl.BlockSpec(memory_space=pl.ANY),
        scratch_shapes=[
            pltpu.VMEM((NJ, WINDOW, JC, cols), bf16),
            pltpu.VMEM((OWN, B, cols), bf16),
            pltpu.VMEM((BAND, JC, B), bf16),
            pltpu.VMEM((JOBS, 4, 2, SHARE, HALF, B), bf16),
            pltpu.VMEM((JOBS, SHARE, HALF, B), bf16),
            pltpu.VMEM((JOBS, SHARE, HALF, B), bf16),
            pltpu.VMEM((JOBS, 2, SHARE, HALF, B), bf16),
            pltpu.VMEM((JOBS, 2, SHARE, HALF, B), bf16),
            pltpu.VMEM((SHARE, B, B), f32),
            pltpu.VMEM((OWN, SHARE, B, B), bf16),
            pltpu.VMEM((occupation.shape[0] // B, B), f32),
            pltpu.VMEM((1, cols), jnp.int32),
            pltpu.SMEM(pattern.shape, jnp.int32),
            dma((OWN,)), dma((3,)), dma((NJ, WINDOW)),
            dma((NJ, OWN)), dma((NJ, OWN)), dma((NJ, 2)), dma((NJ, 2)),
            *[dma((JOBS,))] * 8,
            dma((OWN,)),
        ],
        compiler_params=pltpu.CompilerParams(
            collective_id=0, has_side_effects=True, vmem_limit_bytes=40 * 2**20
        ),
        cost_estimate=pl.CostEstimate(
            flops=2 * OWN * BAND * B * B * cols, bytes_accessed=4 * 2**20, transcendentals=0
        ),
        name="density_blocks",
    )(
        slab.reshape(OWN, NJ, JC, cols),
        occupation.reshape(-1, B),
        column_band.reshape(1, -1),
        pattern,
    )


def solution(mesh):
    placed = (P("wide", "narrow"), P(), P("narrow"), P("wide", None))
    return jax.shard_map(
        per_device,
        mesh=mesh,
        in_specs=placed,
        out_specs=P("wide", "narrow", None, None),
        check_vma=False,
    )
```

```python
import functools

import jax
import jax.numpy as jnp
from jax import lax
from jax.experimental import pallas as pl
from jax.experimental.pallas import tpu as pltpu
from jax.sharding import PartitionSpec as P

MESH = pl.DeviceIdType.MESH
B = 128
REACH = 8
BAND = 2 * REACH + 1
OWN = 6
WINDOW = OWN + 2 * REACH
NJ = 2
JC = B // NJ
HALF = JC // 2
JOBS = OWN * NJ
SHARE = 3
LAG = 5
FAR_AT = NJ


def kernel(
    n_clusters, slab, occ, band, pattern, out,
    window, scaled, blocks, kept, up_out, up_in, down_out, down_in, total, result,
    occ_v, band_v, pat,
    own_sem, in_sem, near_send, near_recv, core_send, core_recv, far_send, far_recv,
    relay_send, relay_recv, up_send, up_recv, down_send, down_recv, out_sem, hello,
):
    wide = lax.axis_index("wide")
    here = lax.axis_index("narrow")
    n_chips = lax.axis_size("wide") // 2
    n_narrow = lax.axis_size("narrow")
    chip, core = wide // 2, lax.rem(wide, 2)
    outward = 2 * core - 1
    near_chip = lax.rem(chip + outward + n_chips, n_chips)
    far_chip = lax.rem(chip - outward + n_chips, n_chips)
    other = (chip * 2 + 1 - core, here)
    near_other = (near_chip * 2 + 1 - core, here)
    near_same = (near_chip * 2 + core, here)
    far_same = (far_chip * 2 + core, here)
    up = (wide, lax.rem(here + 1, n_narrow))
    down = (wide, lax.rem(here + n_narrow - 1, n_narrow))
    first_0 = jnp.logical_and(chip == 0, core == 0)
    first_1 = jnp.logical_and(chip == 0, core == 1)
    last_1 = jnp.logical_and(chip == n_chips - 1, core == 1)
    far_early = jnp.logical_and(core == 0, jnp.logical_or(chip == 0, chip == n_chips - 1))

    def by_core(zero, one):
        return jnp.where(core == 0, zero, one)

    own = [
        pltpu.make_async_copy(slab.at[:, h], window.at[h, pl.ds(REACH, OWN)], own_sem.at[h])
        for h in range(NJ)
    ]
    small = [
        pltpu.make_async_copy(occ, occ_v, in_sem.at[0]),
        pltpu.make_async_copy(band, band_v, in_sem.at[1]),
        pltpu.make_async_copy(pattern, pat, in_sem.at[2]),
    ]
    for copy in own + small:
        copy.start()

    def signal(sem, device):
        pl.semaphore_signal(sem, inc=1, device_id=device, device_id_type=MESH)

    barrier = pltpu.get_barrier_semaphore()
    signal(barrier, up)
    signal(barrier, down)

    @pl.when(jnp.logical_not(first_0))
    def _():
        signal(barrier, other)

    @pl.when(jnp.logical_not(last_1))
    def _():
        signal(barrier, near_other)
        signal(barrier, near_same)

    @pl.when(first_1)
    def _():
        signal(barrier, far_same)

    pl.semaphore_wait(
        barrier,
        5 - first_0.astype(jnp.int32) - 2 * first_1.astype(jnp.int32) + last_1.astype(jnp.int32),
    )

    @pl.when(first_0)
    def _():
        signal(hello.at[1], other)

    @pl.when(last_1)
    def _():
        signal(hello.at[0], near_other)
        signal(hello.at[0], near_same)

    def remote(src, dst, send_sem, recv_sem, device):
        return pltpu.make_async_remote_copy(
            src_ref=src, dst_ref=dst, send_sem=send_sem, recv_sem=recv_sem,
            device_id=device, device_id_type=MESH,
        )

    def near_copy(h, i):
        n = 2 if i == 0 else 1
        src = by_core(0, 4) if i == 0 else by_core(i + 1, 4 - i)
        dst = by_core(14, 6) if i == 0 else by_core(15 + i, 6 - i)
        return remote(
            slab.at[pl.ds(src, n), h], window.at[h, pl.ds(dst, n)],
            near_send.at[h, i], near_recv.at[h, i], near_other,
        )

    def near_arrived(h, i):
        n = 2 if i == 0 else 1
        at = by_core(6, 14) if i == 0 else by_core(6 - i, 15 + i)
        there = window.at[h, pl.ds(at, n)]
        remote(there, there, near_send.at[h, i], near_recv.at[h, i], near_other).wait_recv()

    def core_copy(h):
        return remote(
            slab.at[:, h], window.at[h, pl.ds(by_core(2, 14), OWN)],
            core_send.at[h], core_recv.at[h], other,
        )

    def core_arrived(h):
        there = window.at[h, pl.ds(by_core(14, 2), OWN)]
        remote(there, there, core_send.at[h], core_recv.at[h], other).wait_recv()

    def far_copy(h):
        return remote(
            slab.at[pl.ds(by_core(4, 0), 2), h], window.at[h, pl.ds(by_core(0, 20), 2)],
            far_send.at[h], far_recv.at[h], far_same,
        )

    def far_arrived(h):
        there = window.at[h, pl.ds(by_core(0, 20), 2)]
        remote(there, there, far_send.at[h], far_recv.at[h], far_same).wait_recv()

    def relay_copy(h):
        return remote(
            window.at[h, pl.ds(by_core(6, 14), 2)], window.at[h, pl.ds(by_core(0, 20), 2)],
            relay_send.at[h], relay_recv.at[h], other,
        )

    def relay_arrived(h):
        there = window.at[h, pl.ds(by_core(20, 0), 2)]
        remote(there, there, relay_send.at[h], relay_recv.at[h], other).wait_recv()

    def all_near():
        for h in range(NJ):
            for i in range(2):
                near_copy(h, i).start()
        for i in range(2, 5):
            for h in range(NJ):
                near_copy(h, i).start()

    def all_far():
        for h in range(NJ):
            far_copy(h).start()

    with jax.named_scope("first_sends"):
        pl.when(jnp.logical_not(first_0))(all_near)
        pl.when(far_early)(all_far)

        @pl.when(first_1)
        def _():
            pl.semaphore_wait(hello.at[1], 1)

        for h in range(NJ):
            core_copy(h).start()

    with jax.named_scope("weights"):
        for copy in small:
            copy.wait()
        table = occ_v[...]
        turned = jnp.transpose(
            jnp.concatenate([table, jnp.zeros((B - table.shape[0], B), jnp.float32)], axis=0)
        )
        bands = band_v[...]
        high, low = bands // B, lax.rem(bands, B)
        at = lax.broadcasted_iota(jnp.int32, (B, bands.shape[1]), 0)
        pick_high = jnp.where(at == high, 1.0, 0.0).astype(jnp.bfloat16)
        rest, found = turned, []
        for _ in range(3):
            piece = rest.astype(jnp.bfloat16)
            rest = rest - piece.astype(jnp.float32)
            found.append(jnp.dot(piece, pick_high, preferred_element_type=jnp.float32))
        looked = (found[2] + found[1]) + found[0]
        weight = jnp.sum(jnp.where(at == low, looked, 0.0), axis=0, keepdims=True)

    with jax.named_scope("scale"):
        for h in range(NJ):
            own[h].wait()
        for c in range(OWN):
            for h in range(NJ):
                rows = window[h, REACH + c].astype(jnp.float32) * weight
                scaled[c, pl.ds(h * JC, JC)] = rows.astype(jnp.bfloat16)

    @pl.when(first_0)
    def _():
        pl.semaphore_wait(hello.at[0], 1)
        all_near()

    def cluster(s):
        return jnp.where(first_1, 2 + s if s < 4 else 5 - s, by_core(OWN - 1 - s, s))

    def wait_rows(s, h):
        if s == 0:
            near_arrived(h, 0)
            relay_copy(h).start()
            near_arrived(h, 1)
            core_arrived(h)

        @pl.when(first_1)
        def _():
            if s == 0:
                near_arrived(h, 2)
                near_arrived(h, 3)
            elif s == 1:
                near_arrived(h, 4)
            elif s == 2:
                far_arrived(h)
            elif s == 4:
                relay_arrived(h)

        @pl.when(jnp.logical_not(first_1))
        def _():
            if s == 0:
                relay_arrived(h)
            elif s <= 3:
                near_arrived(h, s + 1)
            elif s == 4:
                far_arrived(h)

    def compute(job):
        s, h = divmod(job, NJ)
        c = cluster(s)
        right = window[h, pl.ds(c, BAND)].reshape(BAND * JC, -1)
        product = lax.dot_general(
            right, scaled[c], (((1,), (1,)), ((), ())), preferred_element_type=jnp.float32
        )
        blocks[...] = product.astype(jnp.bfloat16).reshape(BAND, JC, B)
        mine = wide * OWN + c
        for r in (2, 1, 3, 0):
            for m in range(SHARE):
                slot = lax.rem(here + r, n_narrow) * SHARE + m
                entry = pat[c, slot] - mine + REACH
                entry = jnp.where(entry < 0, entry + n_clusters, entry)
                entry = jnp.where(entry >= n_clusters, entry - n_clusters, entry)
                block = blocks[jnp.clip(entry, 0, BAND - 1)]
                one, two = block[:HALF], block[HALF:]
                if r == 2:
                    up_out[job, 0, m] = one
                    down_out[job, 0, m] = two
                elif r == 1:
                    up_out[job + LAG, 1, m] = one
                    up_out[job + LAG, 2, m] = two
                elif r == 3:
                    down_out[job + LAG, 2, m] = one
                    down_out[job + LAG, 1, m] = two
                else:
                    kept[job, 0, m] = one
                    kept[job, 1, m] = two

    def message(t, src, dst, send_sem, recv_sem, device):
        first, last = (0 if t < JOBS else 1), (3 if t >= LAG else 1)
        part = pl.ds(first, last - first)
        return remote(src.at[t, part], dst.at[t, part], send_sem.at[t], recv_sem.at[t], device)

    def up_message(t):
        return message(t, up_out, up_in, up_send, up_recv, up)

    def down_message(t):
        return message(t, down_out, down_in, down_send, down_recv, down)

    def add_first(t):
        for src, dst in ((up_in, up_out), (down_in, down_out)):
            dst[t, 1] = (
                dst[t, 1].astype(jnp.float32) + src[t - LAG, 0].astype(jnp.float32)
            ).astype(jnp.bfloat16)

    def finish(t):
        job = t - LAG
        s, h = divmod(job, NJ)
        c = cluster(s)
        for half in range(2):
            total[:, pl.ds(h * JC + half * HALF, HALF)] = (
                kept[job, half].astype(jnp.float32)
                + up_in[t, 1 + half].astype(jnp.float32)
                + down_in[t, 2 - half].astype(jnp.float32)
            )
        if h == NJ - 1:
            for m in range(SHARE):
                result[c, m] = jnp.transpose(total[m]).astype(jnp.bfloat16)
            pltpu.make_async_copy(result.at[c], out.at[c], out_sem.at[s]).start()

    for t in range(JOBS + 2 * LAG):
        if t < JOBS:
            with jax.named_scope("wait_rows"):
                wait_rows(*divmod(t, NJ))
            with jax.named_scope("blocks"):
                compute(t)
        if t >= LAG:
            with jax.named_scope("wait_parts"):
                up_message(t - LAG).wait_recv()
                down_message(t - LAG).wait_recv()
        if t < JOBS + LAG:
            with jax.named_scope("send_parts"):
                if t >= LAG:
                    add_first(t)
                up_message(t).start()
                down_message(t).start()
        if t == FAR_AT:

            @pl.when(first_1)
            def _():
                pl.semaphore_wait(hello.at[0], 1)

            pl.when(jnp.logical_not(far_early))(all_far)
        if t >= 2 * LAG:
            with jax.named_scope("finish"):
                finish(t - LAG)

    with jax.named_scope("drain"):
        for h in range(NJ):
            for i in range(5):
                near_copy(h, i).wait_send()
            core_copy(h).wait_send()
            far_copy(h).wait_send()
            relay_copy(h).wait_send()
        for t in range(JOBS + LAG):
            up_message(t).wait_send()
            down_message(t).wait_send()
        for s in range(OWN):
            c = cluster(s)
            pltpu.make_async_copy(result.at[c], out.at[c], out_sem.at[s]).wait()


def per_device(slab, occupation, column_band, pattern):
    cols = slab.shape[1]
    n_clusters = OWN * lax.axis_size("wide")
    dma = pltpu.SemaphoreType.DMA
    bf16, f32 = jnp.bfloat16, jnp.float32
    return pl.pallas_call(
        functools.partial(kernel, n_clusters),
        out_shape=jax.ShapeDtypeStruct((OWN, SHARE, B, B), bf16),
        in_specs=[pl.BlockSpec(memory_space=pl.ANY)] * 4,
        out_specs=pl.BlockSpec(memory_space=pl.ANY),
        scratch_shapes=[
            pltpu.VMEM((NJ, WINDOW, JC, cols), bf16),
            pltpu.VMEM((OWN, B, cols), bf16),
            pltpu.VMEM((BAND, JC, B), bf16),
            pltpu.VMEM((JOBS, 2, SHARE, HALF, B), bf16),
            *[pltpu.VMEM((JOBS + LAG, 3, SHARE, HALF, B), bf16)] * 4,
            pltpu.VMEM((SHARE, B, B), f32),
            pltpu.VMEM((OWN, SHARE, B, B), bf16),
            pltpu.VMEM((occupation.shape[0] // B, B), f32),
            pltpu.VMEM((1, cols), jnp.int32),
            pltpu.SMEM(pattern.shape, jnp.int32),
            dma((NJ,)), dma((3,)), dma((NJ, 5)), dma((NJ, 5)),
            *[dma((NJ,))] * 6,
            *[dma((JOBS + LAG,))] * 4,
            dma((OWN,)), pltpu.SemaphoreType.REGULAR((2,)),
        ],
        compiler_params=pltpu.CompilerParams(
            collective_id=0, has_side_effects=True, vmem_limit_bytes=60 * 2**20
        ),
        cost_estimate=pl.CostEstimate(
            flops=2 * OWN * BAND * B * B * cols, bytes_accessed=4 * 2**20, transcendentals=0
        ),
        name="density_blocks",
    )(
        slab.reshape(OWN, NJ, JC, cols),
        occupation.reshape(-1, B),
        column_band.reshape(1, -1),
        pattern,
    )


def solution(mesh):
    placed = (P("wide", "narrow"), P(), P("narrow"), P("wide", None))
    return jax.shard_map(
        per_device,
        mesh=mesh,
        in_specs=placed,
        out_specs=P("wide", "narrow", None, None),
        check_vma=False,
    )
```

```python
import functools

import jax
import jax.numpy as jnp
from jax import lax
from jax.experimental import pallas as pl
from jax.experimental.pallas import tpu as pltpu
from jax.sharding import PartitionSpec as P

MESH = pl.DeviceIdType.MESH
B = 128
REACH = 8
BAND = 2 * REACH + 1
OWN = 6
WINDOW = OWN + 2 * REACH
NJ = 2
JC = B // NJ
HALF = JC // 2
JOBS = OWN * NJ
SHARE = 3
LAG = 5


def kernel(
    n_clusters, slab, occ, band, pattern, out,
    window, scaled, blocks, kept, up_out, up_in, down_out, down_in, total, result,
    occ_v, band_v, pat,
    own_sem, in_sem, near_send, near_recv, core_send, core_recv, far_send, far_recv,
    relay_send, relay_recv, up_send, up_recv, down_send, down_recv, out_sem, hello,
):
    wide = lax.axis_index("wide")
    here = lax.axis_index("narrow")
    n_chips = lax.axis_size("wide") // 2
    n_narrow = lax.axis_size("narrow")
    chip, core = wide // 2, lax.rem(wide, 2)
    outward = 2 * core - 1
    near_chip = lax.rem(chip + outward + n_chips, n_chips)
    other = (chip * 2 + 1 - core, here)
    near_other = (near_chip * 2 + 1 - core, here)
    up = (wide, lax.rem(here + 1, n_narrow))
    down = (wide, lax.rem(here + n_narrow - 1, n_narrow))
    first_0 = jnp.logical_and(chip == 0, core == 0)
    first_1 = jnp.logical_and(chip == 0, core == 1)
    last_1 = jnp.logical_and(chip == n_chips - 1, core == 1)

    def by_core(zero, one):
        return jnp.where(core == 0, zero, one)

    own = [
        pltpu.make_async_copy(slab.at[:, h], window.at[h, pl.ds(REACH, OWN)], own_sem.at[h])
        for h in range(NJ)
    ]
    small = [
        pltpu.make_async_copy(occ, occ_v, in_sem.at[0]),
        pltpu.make_async_copy(band, band_v, in_sem.at[1]),
        pltpu.make_async_copy(pattern, pat, in_sem.at[2]),
    ]
    for copy in own + small:
        copy.start()

    def signal(sem, device):
        pl.semaphore_signal(sem, inc=1, device_id=device, device_id_type=MESH)

    barrier = pltpu.get_barrier_semaphore()
    signal(barrier, up)
    signal(barrier, down)

    @pl.when(jnp.logical_not(first_0))
    def _():
        signal(barrier, other)

    @pl.when(jnp.logical_not(last_1))
    def _():
        signal(barrier, near_other)

    pl.semaphore_wait(barrier, 4 - (chip == 0).astype(jnp.int32))

    @pl.when(first_0)
    def _():
        signal(hello.at[1], other)

    @pl.when(last_1)
    def _():
        signal(hello.at[0], near_other)

    def remote(src, dst, send_sem, recv_sem, device):
        return pltpu.make_async_remote_copy(
            src_ref=src, dst_ref=dst, send_sem=send_sem, recv_sem=recv_sem,
            device_id=device, device_id_type=MESH,
        )

    def near_copy(h, i):
        n = 2 if i == 0 else 1
        src = by_core(0, 4) if i == 0 else by_core(i + 1, 4 - i)
        dst = by_core(14, 6) if i == 0 else by_core(15 + i, 6 - i)
        return remote(
            slab.at[pl.ds(src, n), h], window.at[h, pl.ds(dst, n)],
            near_send.at[h, i], near_recv.at[h, i], near_other,
        )

    def near_arrived(h, i):
        n = 2 if i == 0 else 1
        at = by_core(6, 14) if i == 0 else by_core(6 - i, 15 + i)
        there = window.at[h, pl.ds(at, n)]
        remote(there, there, near_send.at[h, i], near_recv.at[h, i], near_other).wait_recv()

    def core_copy(h):
        return remote(
            slab.at[:, h], window.at[h, pl.ds(by_core(2, 14), OWN)],
            core_send.at[h], core_recv.at[h], other,
        )

    def core_arrived(h):
        there = window.at[h, pl.ds(by_core(14, 2), OWN)]
        remote(there, there, core_send.at[h], core_recv.at[h], other).wait_recv()

    def far_copy(h):
        return remote(
            window.at[h, pl.ds(by_core(14, 6), 2)], window.at[h, pl.ds(by_core(20, 0), 2)],
            far_send.at[h], far_recv.at[h], near_other,
        )

    def far_arrived(h):
        there = window.at[h, pl.ds(by_core(0, 20), 2)]
        remote(there, there, far_send.at[h], far_recv.at[h], near_other).wait_recv()

    def relay_copy(h):
        return remote(
            window.at[h, pl.ds(by_core(6, 14), 2)], window.at[h, pl.ds(by_core(0, 20), 2)],
            relay_send.at[h], relay_recv.at[h], other,
        )

    def relay_arrived(h):
        there = window.at[h, pl.ds(by_core(20, 0), 2)]
        remote(there, there, relay_send.at[h], relay_recv.at[h], other).wait_recv()

    def all_near():
        for h in range(NJ):
            for i in range(2):
                near_copy(h, i).start()
        for i in range(2, 5):
            for h in range(NJ):
                near_copy(h, i).start()

    with jax.named_scope("first_sends"):
        pl.when(jnp.logical_not(first_0))(all_near)

        @pl.when(first_1)
        def _():
            pl.semaphore_wait(hello.at[1], 1)

        for h in range(NJ):
            core_copy(h).start()

    with jax.named_scope("weights"):
        for copy in small:
            copy.wait()
        table = occ_v[...]
        turned = jnp.transpose(
            jnp.concatenate([table, jnp.zeros((B - table.shape[0], B), jnp.float32)], axis=0)
        )
        bands = band_v[...]
        high, low = bands // B, lax.rem(bands, B)
        at = lax.broadcasted_iota(jnp.int32, (B, bands.shape[1]), 0)
        pick_high = jnp.where(at == high, 1.0, 0.0).astype(jnp.bfloat16)
        rest, found = turned, []
        for _ in range(3):
            piece = rest.astype(jnp.bfloat16)
            rest = rest - piece.astype(jnp.float32)
            found.append(jnp.dot(piece, pick_high, preferred_element_type=jnp.float32))
        looked = (found[2] + found[1]) + found[0]
        weight = jnp.sum(jnp.where(at == low, looked, 0.0), axis=0, keepdims=True)

    with jax.named_scope("scale"):
        for h in range(NJ):
            own[h].wait()
        for c in range(OWN):
            for h in range(NJ):
                rows = window[h, REACH + c].astype(jnp.float32) * weight
                scaled[c, pl.ds(h * JC, JC)] = rows.astype(jnp.bfloat16)

    @pl.when(first_0)
    def _():
        pl.semaphore_wait(hello.at[0], 1)
        all_near()

    def cluster(s):
        return jnp.where(first_1, 2 + s if s < 4 else 5 - s, by_core(OWN - 1 - s, s))

    def wait_rows(s, h):
        if s == 0:
            near_arrived(h, 0)
            relay_copy(h).start()
            core_arrived(h)
            far_copy(h).start()
            near_arrived(h, 1)

        @pl.when(first_1)
        def _():
            if s == 0:
                near_arrived(h, 2)
                near_arrived(h, 3)
            elif s == 1:
                near_arrived(h, 4)
            elif s == 2:
                far_arrived(h)
            elif s == 4:
                relay_arrived(h)

        @pl.when(jnp.logical_not(first_1))
        def _():
            if s == 0:
                relay_arrived(h)
            elif s <= 3:
                near_arrived(h, s + 1)
            elif s == 4:
                far_arrived(h)

    def compute(job):
        s, h = divmod(job, NJ)
        c = cluster(s)
        right = window[h, pl.ds(c, BAND)].reshape(BAND * JC, -1)
        product = lax.dot_general(
            right, scaled[c], (((1,), (1,)), ((), ())), preferred_element_type=jnp.float32
        )
        blocks[...] = product.astype(jnp.bfloat16).reshape(BAND, JC, B)
        mine = wide * OWN + c
        for r in (2, 1, 3, 0):
            for m in range(SHARE):
                slot = lax.rem(here + r, n_narrow) * SHARE + m
                entry = pat[c, slot] - mine + REACH
                entry = jnp.where(entry < 0, entry + n_clusters, entry)
                entry = jnp.where(entry >= n_clusters, entry - n_clusters, entry)
                block = blocks[jnp.clip(entry, 0, BAND - 1)]
                one, two = block[:HALF], block[HALF:]
                if r == 2:
                    up_out[job, 0, m] = one
                    down_out[job, 0, m] = two
                elif r == 1:
                    up_out[job + LAG, 1, m] = one
                    up_out[job + LAG, 2, m] = two
                elif r == 3:
                    down_out[job + LAG, 2, m] = one
                    down_out[job + LAG, 1, m] = two
                else:
                    kept[job, 0, m] = one
                    kept[job, 1, m] = two

    def message(t, src, dst, send_sem, recv_sem, device):
        first, last = (0 if t < JOBS else 1), (3 if t >= LAG else 1)
        part = pl.ds(first, last - first)
        return remote(src.at[t, part], dst.at[t, part], send_sem.at[t], recv_sem.at[t], device)

    def up_message(t):
        return message(t, up_out, up_in, up_send, up_recv, up)

    def down_message(t):
        return message(t, down_out, down_in, down_send, down_recv, down)

    def add_first(t):
        for src, dst in ((up_in, up_out), (down_in, down_out)):
            dst[t, 1] = (
                dst[t, 1].astype(jnp.float32) + src[t - LAG, 0].astype(jnp.float32)
            ).astype(jnp.bfloat16)

    def finish(t):
        job = t - LAG
        s, h = divmod(job, NJ)
        c = cluster(s)
        for half in range(2):
            total[:, pl.ds(h * JC + half * HALF, HALF)] = (
                kept[job, half].astype(jnp.float32)
                + up_in[t, 1 + half].astype(jnp.float32)
                + down_in[t, 2 - half].astype(jnp.float32)
            )
        if h == NJ - 1:
            for m in range(SHARE):
                result[c, m] = jnp.transpose(total[m]).astype(jnp.bfloat16)
            pltpu.make_async_copy(result.at[c], out.at[c], out_sem.at[s]).start()

    for t in range(JOBS + 2 * LAG):
        if t < JOBS:
            with jax.named_scope("wait_rows"):
                wait_rows(*divmod(t, NJ))
            with jax.named_scope("blocks"):
                compute(t)
        if t >= LAG:
            with jax.named_scope("wait_parts"):
                up_message(t - LAG).wait_recv()
                down_message(t - LAG).wait_recv()
        if t < JOBS + LAG:
            with jax.named_scope("send_parts"):
                if t >= LAG:
                    add_first(t)
                up_message(t).start()
                down_message(t).start()
        if t >= 2 * LAG:
            with jax.named_scope("finish"):
                finish(t - LAG)

    with jax.named_scope("drain"):
        for h in range(NJ):
            for i in range(5):
                near_copy(h, i).wait_send()
            core_copy(h).wait_send()
            far_copy(h).wait_send()
            relay_copy(h).wait_send()
        for t in range(JOBS + LAG):
            up_message(t).wait_send()
            down_message(t).wait_send()
        for s in range(OWN):
            c = cluster(s)
            pltpu.make_async_copy(result.at[c], out.at[c], out_sem.at[s]).wait()


def per_device(slab, occupation, column_band, pattern):
    cols = slab.shape[1]
    n_clusters = OWN * lax.axis_size("wide")
    dma = pltpu.SemaphoreType.DMA
    bf16, f32 = jnp.bfloat16, jnp.float32
    return pl.pallas_call(
        functools.partial(kernel, n_clusters),
        out_shape=jax.ShapeDtypeStruct((OWN, SHARE, B, B), bf16),
        in_specs=[pl.BlockSpec(memory_space=pl.ANY)] * 4,
        out_specs=pl.BlockSpec(memory_space=pl.ANY),
        scratch_shapes=[
            pltpu.VMEM((NJ, WINDOW, JC, cols), bf16),
            pltpu.VMEM((OWN, B, cols), bf16),
            pltpu.VMEM((BAND, JC, B), bf16),
            pltpu.VMEM((JOBS, 2, SHARE, HALF, B), bf16),
            *[pltpu.VMEM((JOBS + LAG, 3, SHARE, HALF, B), bf16)] * 4,
            pltpu.VMEM((SHARE, B, B), f32),
            pltpu.VMEM((OWN, SHARE, B, B), bf16),
            pltpu.VMEM((occupation.shape[0] // B, B), f32),
            pltpu.VMEM((1, cols), jnp.int32),
            pltpu.SMEM(pattern.shape, jnp.int32),
            dma((NJ,)), dma((3,)), dma((NJ, 5)), dma((NJ, 5)),
            *[dma((NJ,))] * 6,
            *[dma((JOBS + LAG,))] * 4,
            dma((OWN,)), pltpu.SemaphoreType.REGULAR((2,)),
        ],
        compiler_params=pltpu.CompilerParams(
            collective_id=0, has_side_effects=True, vmem_limit_bytes=60 * 2**20
        ),
        cost_estimate=pl.CostEstimate(
            flops=2 * OWN * BAND * B * B * cols, bytes_accessed=4 * 2**20, transcendentals=0
        ),
        name="density_blocks",
    )(
        slab.reshape(OWN, NJ, JC, cols),
        occupation.reshape(-1, B),
        column_band.reshape(1, -1),
        pattern,
    )


def solution(mesh):
    placed = (P("wide", "narrow"), P(), P("narrow"), P("wide", None))
    return jax.shard_map(
        per_device,
        mesh=mesh,
        in_specs=placed,
        out_specs=P("wide", "narrow", None, None),
        check_vma=False,
    )
```

```python
import functools

import jax
import jax.numpy as jnp
from jax import lax
from jax.experimental import pallas as pl
from jax.experimental.pallas import tpu as pltpu
from jax.sharding import PartitionSpec as P

MESH = pl.DeviceIdType.MESH
B = 128
REACH = 8
BAND = 2 * REACH + 1
OWN = 6
WINDOW = OWN + 2 * REACH
NJ = 2
JC = B // NJ
HALF = JC // 2
JOBS = OWN * NJ
SHARE = 3
STRAIGHT = 8
LAG = 6
AHEAD = (0, 0, 0, 2, 1, 1, 0, 1, 1, 1, 1, 1)


def kernel(
    n_clusters, slab, occ, band, pattern, out,
    window, scaled, blocks, kept, up_out, up_in, down_out, down_in, total, result,
    occ_v, band_v, pat,
    own_sem, in_sem, near_send, near_recv, core_send, core_recv, far_send, far_recv,
    relay_send, relay_recv, up_send, up_recv, down_send, down_recv,
    up2_send, up2_recv, down2_send, down2_recv, out_sem, hello,
):
    wide = lax.axis_index("wide")
    here = lax.axis_index("narrow")
    n_chips = lax.axis_size("wide") // 2
    n_narrow = lax.axis_size("narrow")
    chip, core = wide // 2, lax.rem(wide, 2)
    outward = 2 * core - 1
    near_chip = lax.rem(chip + outward + n_chips, n_chips)
    other = (chip * 2 + 1 - core, here)
    near_other = (near_chip * 2 + 1 - core, here)
    up = (wide, lax.rem(here + 1, n_narrow))
    down = (wide, lax.rem(here + n_narrow - 1, n_narrow))
    across = (wide, lax.rem(here + 2, n_narrow))
    first_0 = jnp.logical_and(chip == 0, core == 0)
    first_1 = jnp.logical_and(chip == 0, core == 1)
    last_1 = jnp.logical_and(chip == n_chips - 1, core == 1)

    def by_core(zero, one):
        return jnp.where(core == 0, zero, one)

    own = [
        pltpu.make_async_copy(slab.at[:, h], window.at[h, pl.ds(REACH, OWN)], own_sem.at[h])
        for h in range(NJ)
    ]
    small = [
        pltpu.make_async_copy(occ, occ_v, in_sem.at[0]),
        pltpu.make_async_copy(band, band_v, in_sem.at[1]),
        pltpu.make_async_copy(pattern, pat, in_sem.at[2]),
    ]
    for copy in own + small:
        copy.start()

    def signal(sem, device):
        pl.semaphore_signal(sem, inc=1, device_id=device, device_id_type=MESH)

    barrier = pltpu.get_barrier_semaphore()
    signal(barrier, up)
    signal(barrier, down)

    @pl.when(jnp.logical_not(first_0))
    def _():
        signal(barrier, other)

    @pl.when(jnp.logical_not(last_1))
    def _():
        signal(barrier, near_other)

    @pl.when(first_1)
    def _():
        signal(barrier, across)

    pl.semaphore_wait(barrier, 4 - first_0.astype(jnp.int32))

    @pl.when(first_0)
    def _():
        signal(hello.at[1], other)

    @pl.when(last_1)
    def _():
        signal(hello.at[0], near_other)

    def remote(src, dst, send_sem, recv_sem, device):
        return pltpu.make_async_remote_copy(
            src_ref=src, dst_ref=dst, send_sem=send_sem, recv_sem=recv_sem,
            device_id=device, device_id_type=MESH,
        )

    def near_copy(h, i):
        n = 2 if i == 0 else 1
        src = by_core(0, 4) if i == 0 else by_core(i + 1, 4 - i)
        dst = by_core(14, 6) if i == 0 else by_core(15 + i, 6 - i)
        return remote(
            slab.at[pl.ds(src, n), h], window.at[h, pl.ds(dst, n)],
            near_send.at[h, i], near_recv.at[h, i], near_other,
        )

    def near_arrived(h, i):
        n = 2 if i == 0 else 1
        at = by_core(6, 14) if i == 0 else by_core(6 - i, 15 + i)
        there = window.at[h, pl.ds(at, n)]
        remote(there, there, near_send.at[h, i], near_recv.at[h, i], near_other).wait_recv()

    def core_copy(h):
        return remote(
            slab.at[:, h], window.at[h, pl.ds(by_core(2, 14), OWN)],
            core_send.at[h], core_recv.at[h], other,
        )

    def core_arrived(h):
        there = window.at[h, pl.ds(by_core(14, 2), OWN)]
        remote(there, there, core_send.at[h], core_recv.at[h], other).wait_recv()

    def far_copy(h):
        return remote(
            window.at[h, pl.ds(by_core(14, 6), 2)], window.at[h, pl.ds(by_core(20, 0), 2)],
            far_send.at[h], far_recv.at[h], near_other,
        )

    def far_arrived(h):
        there = window.at[h, pl.ds(by_core(0, 20), 2)]
        remote(there, there, far_send.at[h], far_recv.at[h], near_other).wait_recv()

    def relay_copy(h):
        return remote(
            window.at[h, pl.ds(by_core(6, 14), 2)], window.at[h, pl.ds(by_core(0, 20), 2)],
            relay_send.at[h], relay_recv.at[h], other,
        )

    def relay_arrived(h):
        there = window.at[h, pl.ds(by_core(20, 0), 2)]
        remote(there, there, relay_send.at[h], relay_recv.at[h], other).wait_recv()

    def all_near():
        for h in range(NJ):
            for i in range(2):
                near_copy(h, i).start()
        for i in range(2, 5):
            for h in range(NJ):
                near_copy(h, i).start()

    with jax.named_scope("first_sends"):
        pl.when(jnp.logical_not(first_0))(all_near)

        @pl.when(first_1)
        def _():
            pl.semaphore_wait(hello.at[1], 1)

        for h in range(NJ):
            core_copy(h).start()

    with jax.named_scope("weights"):
        for copy in small:
            copy.wait()
        table = occ_v[...]
        turned = jnp.transpose(
            jnp.concatenate([table, jnp.zeros((B - table.shape[0], B), jnp.float32)], axis=0)
        )
        bands = band_v[...]
        high, low = bands // B, lax.rem(bands, B)
        at = lax.broadcasted_iota(jnp.int32, (B, bands.shape[1]), 0)
        pick_high = jnp.where(at == high, 1.0, 0.0).astype(jnp.bfloat16)
        rest, found = turned, []
        for _ in range(3):
            piece = rest.astype(jnp.bfloat16)
            rest = rest - piece.astype(jnp.float32)
            found.append(jnp.dot(piece, pick_high, preferred_element_type=jnp.float32))
        looked = (found[2] + found[1]) + found[0]
        weight = jnp.sum(jnp.where(at == low, looked, 0.0), axis=0, keepdims=True)

    with jax.named_scope("scale"):
        for h in range(NJ):
            own[h].wait()
        for c in range(OWN):
            for h in range(NJ):
                rows = window[h, REACH + c].astype(jnp.float32) * weight
                scaled[c, pl.ds(h * JC, JC)] = rows.astype(jnp.bfloat16)

    @pl.when(first_0)
    def _():
        pl.semaphore_wait(hello.at[0], 1)
        all_near()

    for h in range(NJ):
        core_arrived(h)
        far_copy(h).start()

    def wait_rows(s, h, inner_last):
        if s == 0:
            near_arrived(h, 0)
            relay_copy(h).start()
            near_arrived(h, 1)
        if inner_last:
            if s == 0:
                near_arrived(h, 2)
                near_arrived(h, 3)
            elif s == 1:
                near_arrived(h, 4)
            elif s == 2:
                far_arrived(h)
            elif s == 4:
                relay_arrived(h)
        elif s == 0:
            relay_arrived(h)
        elif s <= 3:
            near_arrived(h, s + 1)
        elif s == 4:
            far_arrived(h)

    def compute(job, cluster):
        s, h = divmod(job, NJ)
        c = cluster(s)
        right = window[h, pl.ds(c, BAND)].reshape(BAND * JC, -1)
        product = lax.dot_general(
            right, scaled[c], (((1,), (1,)), ((), ())), preferred_element_type=jnp.float32
        )
        blocks[...] = product.astype(jnp.bfloat16).reshape(BAND, JC, B)
        mine = wide * OWN + c
        for r in (2, 1, 3, 0):
            for m in range(SHARE):
                slot = lax.rem(here + r, n_narrow) * SHARE + m
                entry = pat[c, slot] - mine + REACH
                entry = jnp.where(entry < 0, entry + n_clusters, entry)
                entry = jnp.where(entry >= n_clusters, entry - n_clusters, entry)
                block = blocks[jnp.clip(entry, 0, BAND - 1)]
                one, two = block[:HALF], block[HALF:]
                if r == 2:
                    up_out[job, 0, m] = one
                    down_out[job, 0, m] = two
                elif r == 1:
                    up_out[job + LAG, 1, m] = one
                    up_out[job + LAG, 2, m] = two
                elif r == 3:
                    down_out[job + LAG, 2, m] = one
                    down_out[job + LAG, 1, m] = two
                else:
                    kept[job, 0, m] = one
                    kept[job, 1, m] = two

    def message(t, src, dst, send_sem, recv_sem, device):
        first, last = (0 if t < JOBS else 1), (3 if t >= LAG else 1)
        part = pl.ds(first, last - first)
        return remote(src.at[t, part], dst.at[t, part], send_sem.at[t], recv_sem.at[t], device)

    def up_message(t):
        return message(t, up_out, up_in, up_send, up_recv, up)

    def down_message(t):
        return message(t, down_out, down_in, down_send, down_recv, down)

    def add_first(t):
        for src, dst in ((up_in, up_out), (down_in, down_out)):
            dst[t, 1] = (
                dst[t, 1].astype(jnp.float32) + src[t - LAG, 0].astype(jnp.float32)
            ).astype(jnp.bfloat16)

    def finish(t, cluster, direct=False):
        job = t - LAG
        s, h = divmod(job, NJ)
        c = cluster(s)
        for half in range(2):
            value = (
                kept[job, half].astype(jnp.float32)
                + up_in[t, 1 + half].astype(jnp.float32)
                + down_in[t, 2 - half].astype(jnp.float32)
            )
            if direct:
                value += (up_in if half == 0 else down_in)[job, 0].astype(jnp.float32)
            total[:, pl.ds(h * JC + half * HALF, HALF)] = value
        if h == NJ - 1:
            for m in range(SHARE):
                result[c, m] = jnp.transpose(total[m]).astype(jnp.bfloat16)
            pltpu.make_async_copy(result.at[c], out.at[c], out_sem.at[s]).start()

    def results_written(cluster):
        for s in range(OWN):
            c = cluster(s)
            pltpu.make_async_copy(result.at[c], out.at[c], out_sem.at[s]).wait()

    def outwards():
        def cluster(s):
            return by_core(OWN - 1 - s, s)

        for t in range(JOBS + 2 * LAG):
            if t < JOBS:
                wait_rows(*divmod(t, NJ), False)
                compute(t, cluster)
            if t >= LAG:
                up_message(t - LAG).wait_recv()
                down_message(t - LAG).wait_recv()
            if t < JOBS + LAG:
                if t >= LAG:
                    add_first(t)
                up_message(t).start()
                down_message(t).start()
            if t >= 2 * LAG:
                finish(t - LAG, cluster)
        for t in range(JOBS + LAG):
            up_message(t).wait_send()
            down_message(t).wait_send()
        results_written(cluster)

    def outer_first():
        def cluster(s):
            return 2 + s if s < 4 else 5 - s

        def pair(t, first, n, send, recv):
            part = pl.ds(first, n)
            return (
                remote(up_out.at[t, part], up_in.at[t, part], send[0], recv[0], up),
                remote(down_out.at[t, part], down_in.at[t, part], send[1], recv[1], down),
            )

        def first_pair(job):
            return pair(
                job, 0, 1, (up_send.at[job], down_send.at[job]), (up_recv.at[job], down_recv.at[job])
            )

        def sum_pair(job):
            return pair(
                job + LAG, 1, 2,
                (up2_send.at[job], down2_send.at[job]), (up2_recv.at[job], down2_recv.at[job]),
            )

        def straight(job):
            part = pl.ds(1, 2)
            t = job + LAG
            return (
                remote(up_out.at[job, 0], up_in.at[job, 0], up2_send.at[job], up2_recv.at[job], across),
                remote(down_out.at[job, 0], down_in.at[job, 0], down2_send.at[job], down2_recv.at[job], across),
                remote(up_out.at[t, part], up_in.at[t, part], up_send.at[job], up_recv.at[job], up),
                remote(down_out.at[t, part], down_in.at[t, part], down_send.at[job], down_recv.at[job], down),
            )

        def started(job):
            return straight(job) if job < STRAIGHT else first_pair(job)

        def pass_on(job):
            if job < STRAIGHT:
                return
            for copy in first_pair(job):
                copy.wait_recv()
            add_first(job + LAG)
            for copy in sum_pair(job):
                copy.start()

        def end(job):
            for copy in straight(job) if job < STRAIGHT else sum_pair(job):
                copy.wait_recv()
            finish(job + LAG, cluster, job < STRAIGHT)

        passed = ended = 0
        for t in range(JOBS):
            wait_rows(*divmod(t, NJ), True)
            compute(t, cluster)
            for copy in started(t):
                copy.start()
            for _ in range(AHEAD[t]):
                pass_on(passed)
                passed += 1
            if passed - ended > 5:
                end(ended)
                ended += 1
        while passed < JOBS:
            pass_on(passed)
            passed += 1
            if passed - ended > 5:
                end(ended)
                ended += 1
        for job in range(ended, JOBS):
            end(job)
        for job in range(JOBS):
            for copy in started(job) + (() if job < STRAIGHT else sum_pair(job)):
                copy.wait_send()
        results_written(cluster)

    pl.when(first_1)(outer_first)
    pl.when(jnp.logical_not(first_1))(outwards)

    with jax.named_scope("drain"):
        for h in range(NJ):
            for i in range(5):
                near_copy(h, i).wait_send()
            core_copy(h).wait_send()
            far_copy(h).wait_send()
            relay_copy(h).wait_send()


def per_device(slab, occupation, column_band, pattern):
    cols = slab.shape[1]
    n_clusters = OWN * lax.axis_size("wide")
    dma = pltpu.SemaphoreType.DMA
    bf16, f32 = jnp.bfloat16, jnp.float32
    return pl.pallas_call(
        functools.partial(kernel, n_clusters),
        out_shape=jax.ShapeDtypeStruct((OWN, SHARE, B, B), bf16),
        in_specs=[pl.BlockSpec(memory_space=pl.ANY)] * 4,
        out_specs=pl.BlockSpec(memory_space=pl.ANY),
        scratch_shapes=[
            pltpu.VMEM((NJ, WINDOW, JC, cols), bf16),
            pltpu.VMEM((OWN, B, cols), bf16),
            pltpu.VMEM((BAND, JC, B), bf16),
            pltpu.VMEM((JOBS, 2, SHARE, HALF, B), bf16),
            *[pltpu.VMEM((JOBS + LAG, 3, SHARE, HALF, B), bf16)] * 4,
            pltpu.VMEM((SHARE, B, B), f32),
            pltpu.VMEM((OWN, SHARE, B, B), bf16),
            pltpu.VMEM((occupation.shape[0] // B, B), f32),
            pltpu.VMEM((1, cols), jnp.int32),
            pltpu.SMEM(pattern.shape, jnp.int32),
            dma((NJ,)), dma((3,)), dma((NJ, 5)), dma((NJ, 5)),
            *[dma((NJ,))] * 6,
            *[dma((JOBS + LAG,))] * 4,
            *[dma((JOBS,))] * 4,
            dma((OWN,)), pltpu.SemaphoreType.REGULAR((2,)),
        ],
        compiler_params=pltpu.CompilerParams(
            collective_id=0, has_side_effects=True, vmem_limit_bytes=60 * 2**20
        ),
        cost_estimate=pl.CostEstimate(
            flops=2 * OWN * BAND * B * B * cols, bytes_accessed=4 * 2**20, transcendentals=0
        ),
        name="density_blocks",
    )(
        slab.reshape(OWN, NJ, JC, cols),
        occupation.reshape(-1, B),
        column_band.reshape(1, -1),
        pattern,
    )


def solution(mesh):
    placed = (P("wide", "narrow"), P(), P("narrow"), P("wide", None))
    return jax.shard_map(
        per_device,
        mesh=mesh,
        in_specs=placed,
        out_specs=P("wide", "narrow", None, None),
        check_vma=False,
    )
```
